1024 devices in a mesh: expert: 64 (over z, x), tensor: 16 (over y, core).
Axes of the slice: x: 8, y: 8, z: 8, core: 2. Of those that a mesh axis runs over, the one named last changes fastest.
Arguments:
- routes: int32 [3072, 8], P('expert'), may hold values from 0 to 63, all different within a row; in each aligned block of 48 rows (0 to 47, 48 to 95, ...) at most 9 rows name the same one
- gates: float32 [3072, 8], P('expert'), may hold values from 0.05 to 0.4
- hidden: bfloat16 [64, 576, 3072], P('expert', None, 'tensor'), may hold values from -6 to 6
- down: bfloat16 [64, 3072, 4096], P('expert', None, 'tensor'), may hold values from -0.109375 to 0.109375
- out_grad: bfloat16 [3072, 4096], P('expert', 'tensor'), may hold values from -6 to 6
Outputs:
- mixed: bfloat16 [3072, 4096], P('expert', 'tensor')
- hidden_grad: bfloat16 [64, 576, 3072], P('expert', None, 'tensor')
The draws below stay inside these ranges and needn't reach their ends.
Inputs may be any that keep to these rules, and one draw needn't show every extreme that they name: `routes`: each row names 8 different experts. Within the rows of one token block (48 rows, aligned), no expert is named more than 9 times, a bound that some block reaches.
All inputs are finite; a program needn't handle non-finite values.
Results may differ from the reference program's by a relative error of at most 0.0049.
Values may be sent and summed in bfloat16 or wider, within the bound.
A program may use at most 32 MiB of HBM per device.

```python
import math
import jax
import jax.numpy as jnp
import numpy as np
from jax import lax

D = 4096
FF = 3072
TOPK = 8
TOK_DEV = 48
EXPERTS = 64
TOKENS = 3072
CAP = 9


def block_scale(own_key, extent, pieces, least, largest):
    def one(position, shards_of):
        draws = jax.random.uniform(jax.random.fold_in(jax.random.fold_in(own_key, 6), position), (shards_of,), jnp.float32, least / len(pieces), largest / len(pieces))
        return jnp.repeat(jnp.exp(draws), extent[position] // shards_of).reshape((-1,) + (1,) * (len(extent) - position - 1))

    loudness = one(*pieces[0])
    for cut in pieces[1:]:
        loudness = loudness * one(*cut)
    return loudness


def shared_out(stream_key, own, number, rows, amount, top, bound, skew):
    ranking = jax.random.permutation(stream_key, amount)
    packed, usual = portions_of(amount, rows * top, bound, skew, True), portions_of(amount, rows * top, bound, skew, False)
    places = jnp.arange(amount)

    def named(lengths, offset_by):
        used = int((lengths > 0).sum())
        fixed = max(1, used // 4)
        moved = fixed + (places - fixed + offset_by * (used - fixed)) % max(1, amount - fixed)
        return jnp.zeros((amount,), jnp.int32).at[ranking[jnp.where(places < fixed, places, moved)]].set(jnp.asarray(lengths, jnp.int32))

    lengths = jnp.where(number % 4 == 0, named(packed, number // 4), named(usual, number - number // 4 - 1))
    mixed = jax.random.permutation(jax.random.fold_in(own, 3), amount)
    giver, receiver = mixed[0:amount // 2 * 2:2], mixed[1:amount // 2 * 2:2]
    margin = jnp.minimum(lengths[giver] - 1, bound - lengths[receiver]) // 2
    margin = jnp.where((giver == ranking[0]) | (receiver == ranking[0]) | (lengths[receiver] == 0), 0, jnp.maximum(margin, 0))
    moved = jax.random.randint(jax.random.fold_in(own, 4), (amount // 2,), 0, 1 << 20) % (margin + 1)
    lengths = lengths.at[giver].add(-moved).at[receiver].add(moved)
    members = jnp.searchsorted(jnp.cumsum(lengths), jnp.arange(rows * top), side="right").astype(jnp.int32)
    grid = members.reshape(top, rows).T
    grid = grid[jax.random.permutation(jax.random.fold_in(own, 1), rows)]
    offset_by = jax.random.randint(jax.random.fold_in(own, 2), (rows, 1), 0, top)
    return jnp.take_along_axis(grid, (jnp.arange(top)[None, :] + offset_by) % top, axis=1)


def portions_of(amount, total, limit, slope, full):
    portions = [(1 << 20) // math.isqrt(standing ** slope) + 1 for standing in range(1, amount + 1)]
    largest = limit if full else min(limit, max(-(-total // amount), total * portions[0] // sum(portions)))
    least = 1 if total - largest >= amount - 1 else 0
    holding, rest = [largest] + [least] * (amount - 1), total - largest - least * (amount - 1)
    while rest > 0:
        movable = [i for i in range(1, amount) if holding[i] < largest] or [i for i in range(1, amount) if holding[i] < limit]
        whole, budget = sum([portions[i] for i in movable]), rest
        for i in movable:
            extra = min(limit - holding[i], max(1, budget * portions[i] // whole), rest)
            holding[i] = holding[i] + extra
            rest = rest - extra
    return np.array(holding)


def normal_values(own_key, extent, deviation, most, shards=(), kind=jnp.bfloat16):
    entries = deviation * jax.random.normal(own_key, extent, jnp.float32)
    if shards:
        entries = entries * block_scale(own_key, extent, shards, -0.22, 0.18)
    return jnp.clip(entries, -most, most).astype(kind)


def setup_inputs(seed: int = 0) -> dict:
    splits = jax.random.split(jax.random.key(seed), 6)
    routes_keys = jax.random.split(jax.random.fold_in(splits[0], 1), TOKENS // TOK_DEV)
    routes_turns = jax.random.permutation(jax.random.fold_in(splits[0], 3), TOKENS // TOK_DEV)
    routes = jax.vmap(lambda own, number: shared_out(jax.random.fold_in(splits[0], 2), own, number, TOK_DEV, EXPERTS, TOPK, CAP, 2))(routes_keys, routes_turns).reshape((TOKENS, TOPK))
    gates = jnp.clip(0.05 + 0.35 * jax.random.uniform(splits[1], (TOKENS, TOPK), jnp.float32) ** block_scale(splits[1], (TOKENS, TOPK), ((0, 64),), -0.2, 0.2), 0.05, 0.4)
    hidden = normal_values(splits[2], (EXPERTS, EXPERTS * CAP, FF), 1.0, 6.0, ((0, 64), (2, 16)))
    down = normal_values(splits[3], (EXPERTS, FF, D), FF ** -0.5, 0.109375, ((0, 64), (2, 16)))
    out_grad = normal_values(splits[4], (TOKENS, D), 1.0, 6.0, ((0, 64), (1, 16)))
    return {"routes": routes, "gates": gates, "hidden": hidden, "down": down, "out_grad": out_grad}


def slot_numbers(block_routes, count):
    flat_index = block_routes.reshape(-1)
    onehot = (flat_index[:, None] == jnp.arange(count, dtype=jnp.int32)[None, :]).astype(jnp.int32)
    before = jnp.cumsum(onehot, axis=0) - onehot
    return jnp.sum(before * onehot, axis=1).reshape(block_routes.shape).astype(jnp.int32)


def forward_one(operands):
    return jnp.dot(operands[0], operands[1], preferred_element_type=jnp.float32).astype(jnp.bfloat16)


def backward_one(operands):
    return lax.dot_general(operands[0], operands[1], (((1,), (1,)), ((), ())), preferred_element_type=jnp.float32).astype(jnp.bfloat16)


def reference(routes, gates, hidden, down, out_grad):
    block_count = TOKENS // TOK_DEV
    block_routes = routes.reshape(block_count, TOK_DEV, TOPK)
    slot = jax.vmap(lambda r: slot_numbers(r, EXPERTS))(block_routes).reshape(TOKENS, TOPK)
    block_of = (jnp.arange(TOKENS, dtype=jnp.int32) // TOK_DEV)[:, None]
    row_index = (block_of * CAP + slot).astype(jnp.int32)
    expert_out = lax.map(forward_one, (hidden, down))
    gathered_out = expert_out[routes, row_index]
    mixed = jnp.sum(gates[:, :, None] * gathered_out.astype(jnp.float32), axis=1).astype(jnp.bfloat16)
    scaled = (gates[:, :, None] * out_grad.astype(jnp.float32)[:, None, :]).astype(jnp.bfloat16)
    routed_grad = jnp.zeros((EXPERTS, EXPERTS * CAP, D), jnp.bfloat16).at[routes, row_index].set(scaled)
    hidden_grad = lax.map(backward_one, (routed_grad, down))
    return mixed, hidden_grad
```

```python
import functools

import jax
import jax.numpy as jnp
from jax import lax
from jax.experimental import pallas as pl
from jax.experimental.pallas import tpu as pltpu
from jax.sharding import PartitionSpec as P

MESH = pl.DeviceIdType.MESH
GROUP = 16
BF, F32 = jnp.bfloat16, jnp.float32


def dot(a, b):
    return jnp.dot(a, b, preferred_element_type=F32)


def dot_nt(a, b):
    return lax.dot_general(a, b, (((1,), (1,)), ((), ())), preferred_element_type=F32)


def iota(shape, axis):
    return lax.broadcasted_iota(jnp.int32, shape, axis)


def kernel(
    sizes,
    routes_ref, gates_ref, grad_ref, hidden_ref, down_ref,
    mixed_ref, hgrad_ref,
    hin, wext, ring, acc_own, acc_sib, sib_in, rg,
    part, rs_out, rs_in, send_g, recv_g, send_e, recv_e,
    local_sem, ag_send, ag_recv, rs_send, rs_recv, sib_send, sib_recv, a2a_send, a2a_recv,
):
    ne, ny, cap, tok, top, rows, cols, feat = sizes
    half, quarter = rows // 2, rows // 4
    wide = 2 * cols
    pad = 256 - cols
    span = ne * GROUP
    me = lax.axis_index("expert")
    tt = lax.axis_index("tensor")
    y, core = tt // 2, tt % 2
    right = ((y + 1) % ny) * 2 + core
    left = ((y + ny - 1) % ny) * 2 + core
    other = y * 2 + (1 - core)

    copy_h = pltpu.make_async_copy(hidden_ref, hin, local_sem.at[0])
    copy_w = pltpu.make_async_copy(
        down_ref.at[:, core], wext.at[:, pl.ds(pad, cols), pl.ds(0, feat)], local_sem.at[1]
    )
    copy_h.start()
    copy_w.start()

    barrier = pltpu.get_barrier_semaphore()

    def greet(i, carry):
        pl.semaphore_signal(barrier, inc=1, device_id=((me + i) % ne, tt), device_id_type=MESH)
        return carry

    for peer in (right, left, other):
        pl.semaphore_signal(barrier, inc=1, device_id=(me, peer), device_id_type=MESH)
    lax.fori_loop(1, ne, greet, 0)

    wext[:, 0:pad, :] = jnp.zeros((ny, pad, 2 * feat), BF)
    wext[:, pad + cols :, :] = jnp.zeros((ny, pad, 2 * feat), BF)

    copy_h.wait()
    ring[0, :, 0:cols] = hin[0:half, :]
    ring[0, :, cols:wide] = hin[half:rows, :]

    pl.semaphore_wait(barrier, ne - 1 + 3)

    def remote(src, dst, send, recv, peer):
        return pltpu.make_async_remote_copy(
            src_ref=src, dst_ref=dst, send_sem=send, recv_sem=recv, device_id=(me, peer), device_id_type=MESH
        )

    copy_ws = remote(
        down_ref.at[:, 1 - core],
        wext.at[:, pl.ds(pad, cols), pl.ds(feat, feat)],
        sib_send.at[0],
        sib_recv.at[0],
        other,
    )
    copy_ws.start()

    def ag_place(way, i):
        step, which = i // 2, (i % 2) ^ way
        src, dst = (step, step + 1) if way == 0 else ((ny - step) % ny, ny - 1 - step)
        return src, dst, which

    ag = []
    for way in range(2):
        ag.append([])
        for i in range(ny - 1):
            src, dst, which = ag_place(way, i)
            chunk = pl.ds(which * quarter, quarter)
            ag[way].append(
                remote(ring.at[src, chunk], ring.at[dst, chunk], ag_send.at[way, i], ag_recv.at[way, i], (right, left)[way])
            )
    for i in range(2):
        for way in range(2):
            ag[way][i].start()

    with jax.named_scope("routing"):
        named = jnp.zeros((tok, ne), F32)
        gate = jnp.zeros((tok, ne), F32)
        for k in range(top):
            hit = routes_ref[:, k : k + 1] == iota((tok, ne), 1)
            named = named + jnp.where(hit, 1.0, 0.0)
            gate = gate + jnp.where(hit, gates_ref[:, k : k + 1], 0.0)
        earlier = jnp.where(iota((tok, tok), 1) < iota((tok, tok), 0), 1.0, 0.0).astype(BF)
        slot = jnp.where(named > 0.5, dot(earlier, named.astype(BF)), 100.0).astype(BF)
        gate_1 = gate.astype(BF)
        gate_2 = (gate - gate_1.astype(F32)).astype(BF)
        gate_3 = (gate - gate_1.astype(F32) - gate_2.astype(F32)).astype(BF)
        gate_of = (gate_1, gate_2, gate_3)

        spread = jnp.where(iota((span, ne), 0) // GROUP == iota((span, ne), 1), 1.0, 0.0).astype(BF)
        place = (iota((span, tok), 0) % GROUP).astype(F32)
        takes = dot_nt(spread, slot) == place
        gate_rows = dot_nt(spread, gate_1) + dot_nt(spread, gate_2) + dot_nt(spread, gate_3)
        gate_rows = jnp.sum(jnp.where(takes, gate_rows, 0.0), axis=1, keepdims=True)
        takes = jnp.where(takes, 1.0, 0.0).astype(BF)
        send_g[...] = (dot(takes, grad_ref[...]) * gate_rows).astype(BF)

    def group(e):
        return pl.ds(pl.multiple_of(e * GROUP, GROUP), GROUP)

    def exchange(src, dst, n):
        def one(i, carry):
            peer = (me + i) % ne
            pltpu.make_async_remote_copy(
                src_ref=src.at[group(peer)],
                dst_ref=dst.at[group(me)],
                send_sem=a2a_send.at[n],
                recv_sem=a2a_recv.at[n],
                device_id=(peer, tt),
                device_id_type=MESH,
            ).start()
            return carry

        lax.fori_loop(1, ne, one, 0)
        dst[group(me), :] = src[group(me), :]

    def exchanged(src, dst, n):
        all_but_one = pl.ds(0, span - GROUP)
        return remote(src.at[all_but_one], dst.at[all_but_one], a2a_send.at[n], a2a_recv.at[n], other)

    exchange(send_g, recv_g, 0)

    packed, padded = GROUP * cap, GROUP * GROUP

    def selection(row, col):
        return jnp.where((row == cap * (col // GROUP) + col % GROUP) & (col % GROUP < cap), 1.0, 0.0).astype(BF)

    compact = selection(iota((packed, padded), 0), iota((packed, padded), 1))
    expand = selection(iota((padded, packed), 1), iota((padded, packed), 0))

    copy_w.wait()
    copy_ws.wait_recv()

    def forward(d, which, first):
        weights = wext.at[(y + ny - d) % ny]
        chunk = slice(which * quarter, (which + 1) * quarter)
        for part_no, lanes, depth in ((0, slice(0, 256), slice(pad, pad + 256)), (1, slice(wide - 256, wide), slice(0, 256))):
            out = slice(part_no * half + which * quarter, part_no * half + (which + 1) * quarter)
            block = ring[d, chunk, lanes]
            own = dot(block, weights[depth, 0:feat])
            sib = dot(block, weights[depth, feat:])
            acc_own[out, :] = own if first else acc_own[out, :] + own
            acc_sib[out, :] = sib if first else acc_sib[out, :] + sib

    for which in range(2):
        forward(0, which, True)
    for i in range(ny - 3):
        for way in range(2):
            ag[way][i].wait_recv()
            ag[way][i + 2].start()
        for way in range(2):
            _, dst, which = ag_place(way, i)
            forward(dst, which, False)

    exchanged(send_g, recv_g, 0).wait_recv()
    for b in range(ne // GROUP):
        rg[b * packed : (b + 1) * packed, 0:feat] = dot(compact, recv_g[b * padded : (b + 1) * padded, :]).astype(BF)
    copy_rg = remote(rg.at[:, pl.ds(0, feat)], rg.at[:, pl.ds(feat, feat)], sib_send.at[1], sib_recv.at[1], other)
    copy_rg.start()

    for i in range(ny - 3, ny - 1):
        for way in range(2):
            ag[way][i].wait_recv()
            _, dst, which = ag_place(way, i)
            forward(dst, which, False)
    copy_e = remote(acc_sib, sib_in, sib_send.at[2], sib_recv.at[2], other)
    copy_e.start()

    def backward(d):
        weights = wext.at[(y + d) % ny]
        low = dot_nt(rg[0:half, :], weights[pad : pad + 256, :])
        high = dot_nt(rg[half:rows, :], weights[0:256, :])
        part[d, :, 0:128] = low[:, 0:128]
        part[d, :, 128:256] = low[:, 128:256] + high[:, 0:128]
        part[d, :, 256:384] = high[:, 128:256]

    far = ny // 2
    rs, rs_place = [], []
    for way in range(2):
        places = [(far, way)]
        for step in range(1, far):
            d = far - step if way == 0 else far + step
            places += [(d, 1 - way), (d, way)]
        rs_place.append(places + [(0, 1 - way), (0, way)])
        rs.append(
            [
                remote(rs_out.at[way, i], rs_in.at[way, i], rs_send.at[way, i], rs_recv.at[way, i], (right, left)[way])
                for i in range(ny - 1)
            ]
        )

    def rs_step(way, i):
        d, which = rs_place[way][i]
        total = part[d, which * quarter : (which + 1) * quarter, :]
        if i >= 2:
            rs[way][i - 2].wait_recv()
            total = total + rs_in[way, i - 2].astype(F32)
        rs_out[way, i] = total.astype(BF)
        rs[way][i].start()

    copy_rg.wait_recv()
    backward(far)
    rs_step(0, 0)
    rs_step(1, 0)
    backward(far - 1)
    rs_step(0, 1)
    backward(far + 1)
    rs_step(1, 1)

    copy_e.wait_recv()
    for b in range(ne // GROUP):
        block = slice(b * packed, (b + 1) * packed)
        total = (acc_own[block, :] + sib_in[block, :]).astype(BF)
        send_e[b * padded : (b + 1) * padded, :] = dot(expand, total).astype(BF)
    exchange(send_e, recv_e, 1)

    done = {far, far - 1, far + 1}
    for i in range(2, ny - 1):
        for way in range(2):
            d, _ = rs_place[way][i]
            if d not in done:
                backward(d)
                done.add(d)
        for way in range(2):
            rs_step(way, i)
    backward(0)

    with jax.named_scope("combine"):
        spread_t = jnp.where(iota((ne, span), 1) // GROUP == iota((ne, span), 0), 1.0, 0.0).astype(BF)
        place_t = (iota((tok, span), 1) % GROUP).astype(F32)
        takes_t = dot(slot, spread_t) == place_t
        mixing = [jnp.where(takes_t, dot(g, spread_t), 0.0).astype(BF) for g in gate_of]
        exchanged(send_e, recv_e, 1).wait_recv()
        mixed_ref[...] = (
            dot(mixing[0], recv_e[...]) + dot(mixing[1], recv_e[...]) + dot(mixing[2], recv_e[...])
        ).astype(BF)

    rs_own = [None, None]
    for i in range(ny - 3, ny - 1):
        for way in range(2):
            _, which = rs_place[way][i + 2]
            rs[way][i].wait_recv()
            if rs_own[which] is None:
                rs_own[which] = part[0, which * quarter : (which + 1) * quarter, :]
            rs_own[which] = rs_own[which] + rs_in[way, i].astype(F32)
    for which in range(2):
        total = rs_own[which].astype(BF)
        hgrad_ref[which * quarter : (which + 1) * quarter, :] = total[:, 0:cols]
        hgrad_ref[half + which * quarter : half + (which + 1) * quarter, :] = total[:, cols:wide]

    for way in range(2):
        for i in range(ny - 1):
            ag[way][i].wait_send()
            rs[way][i].wait_send()
    for copy in (copy_ws, copy_rg, copy_e):
        copy.wait_send()
    exchanged(send_g, recv_g, 0).wait_send()
    exchanged(send_e, recv_e, 1).wait_send()


def body(routes, gates, hidden, down, out_grad):
    ne, nt = lax.axis_size("expert"), lax.axis_size("tensor")
    ny = nt // 2
    tok, top = routes.shape
    rows, cols = hidden.shape[1:]
    feat = out_grad.shape[1]
    cap = rows // ne
    sizes = (ne, ny, cap, tok, top, rows, cols, feat)
    half, quarter, wide = rows // 2, rows // 4, 2 * cols
    span = ne * GROUP
    vmem, anywhere = pl.BlockSpec(memory_space=pltpu.VMEM), pl.BlockSpec(memory_space=pl.ANY)
    dma = pltpu.SemaphoreType.DMA
    mixed, hgrad = pl.pallas_call(
        functools.partial(kernel, sizes),
        out_shape=(
            jax.ShapeDtypeStruct((tok, feat), BF),
            jax.ShapeDtypeStruct((rows, cols), BF),
        ),
        in_specs=[vmem, vmem, vmem, anywhere, anywhere],
        out_specs=(vmem, vmem),
        scratch_shapes=[
            pltpu.VMEM((rows, cols), BF),
            pltpu.VMEM((ny, 512 - cols, 2 * feat), BF),
            pltpu.VMEM((ny, half, wide), BF),
            pltpu.VMEM((rows, feat), F32),
            pltpu.VMEM((rows, feat), F32),
            pltpu.VMEM((rows, feat), F32),
            pltpu.VMEM((rows, 2 * feat), BF),
            pltpu.VMEM((ny, half, wide), F32),
            pltpu.VMEM((2, ny - 1, quarter, wide), BF),
            pltpu.VMEM((2, ny - 1, quarter, wide), BF),
            pltpu.VMEM((span, feat), BF),
            pltpu.VMEM((span, feat), BF),
            pltpu.VMEM((span, feat), BF),
            pltpu.VMEM((span, feat), BF),
            dma((2,)),
            dma((2, ny - 1)),
            dma((2, ny - 1)),
            dma((2, ny - 1)),
            dma((2, ny - 1)),
            dma((3,)),
            dma((3,)),
            dma((2,)),
            dma((2,)),
        ],
        compiler_params=pltpu.CompilerParams(
            collective_id=0, has_side_effects=True, vmem_limit_bytes=48 * 1024 * 1024
        ),
    )(routes, gates, out_grad, hidden[0], down.reshape(ny, 2, cols, feat))
    return mixed, hgrad[None]


def solution(mesh):
    return jax.shard_map(
        body,
        mesh=mesh,
        in_specs=(
            P("expert", None),
            P("expert", None),
            P("expert", None, "tensor"),
            P("expert", None, "tensor"),
            P("expert", "tensor"),
        ),
        out_specs=(P("expert", "tensor"), P("expert", None, "tensor")),
        check_vma=False,
    )
```

```python
import functools

import jax
import jax.numpy as jnp
from jax import lax
from jax.experimental import pallas as pl
from jax.experimental.pallas import tpu as pltpu
from jax.sharding import PartitionSpec as P

MESH = pl.DeviceIdType.MESH
GROUP = 16
STRIDE, HALF_STRIDE = 27, 11
BF, F32 = jnp.bfloat16, jnp.float32


def dot(a, b):
    return jnp.dot(a, b, preferred_element_type=F32)


def dot_nt(a, b):
    return lax.dot_general(a, b, (((1,), (1,)), ((), ())), preferred_element_type=F32)


def iota(shape, axis):
    return lax.broadcasted_iota(jnp.int32, shape, axis)


def kernel(
    sizes,
    routes_hbm, gates_hbm, grad_hbm, hidden_hbm, down_hbm,
    mixed_ref, hgrad_ref,
    routes_ref, gates_ref, grad_ref, hin, wext, ring, acc_own, acc_sib, sib_in, rg,
    part, rs_out, rs_in, send_g, recv_g, send_e, recv_e,
    local_sem, ag_send, ag_recv, rs_send, rs_recv, sib_send, sib_recv, a2a_send, a2a_recv,
):
    ne, ny, cap, tok, top, rows, cols, feat = sizes
    half, quarter = rows // 2, rows // 4
    wide = 2 * cols
    pad = 256 - cols
    span = ne * GROUP
    cut = (quarter // 2 + 15) // 16 * 16
    subs = ((0, cut), (cut, quarter - cut))
    me = lax.axis_index("expert")
    tt = lax.axis_index("tensor")
    y, core = tt // 2, tt % 2
    right = ((y + 1) % ny) * 2 + core
    left = ((y + ny - 1) % ny) * 2 + core
    other = y * 2 + (1 - core)

    copy_h = pltpu.make_async_copy(hidden_hbm, hin, local_sem.at[0])
    copy_r = pltpu.make_async_copy(routes_hbm, routes_ref, local_sem.at[1])
    copy_k = pltpu.make_async_copy(gates_hbm, gates_ref, local_sem.at[2])
    copy_o = pltpu.make_async_copy(grad_hbm, grad_ref, local_sem.at[3])
    copy_w = pltpu.make_async_copy(
        down_hbm.at[:, core], wext.at[:, pl.ds(pad, cols), pl.ds(0, feat)], local_sem.at[4]
    )
    for copy in (copy_h, copy_r, copy_k, copy_o, copy_w):
        copy.start()

    barrier = pltpu.get_barrier_semaphore()

    def greet(i, carry):
        pl.semaphore_signal(barrier, inc=1, device_id=((me + i) % ne, tt), device_id_type=MESH)
        return carry

    for peer in (right, left, other):
        pl.semaphore_signal(barrier, inc=1, device_id=(me, peer), device_id_type=MESH)
    lax.fori_loop(1, ne, greet, 0)

    wext[:, 0:pad, :] = jnp.zeros((ny, pad, 2 * feat), BF)
    wext[:, pad + cols :, :] = jnp.zeros((ny, pad, 2 * feat), BF)

    copy_h.wait()
    own_rows = jnp.transpose(hin[...])
    for q in range(4):
        g, side = q // 2, q % 2
        ring[0, g * quarter : (g + 1) * quarter, side * cols : (side + 1) * cols] = own_rows[q * quarter : (q + 1) * quarter, :]

    pl.semaphore_wait(barrier, ne - 1 + 3)

    def remote(src, dst, send, recv, peer):
        return pltpu.make_async_remote_copy(
            src_ref=src, dst_ref=dst, send_sem=send, recv_sem=recv, device_id=(me, peer), device_id_type=MESH
        )

    def ag_place(way, i):
        step, which = i // 2, (i % 2) ^ way
        src, dst = (step, step + 1) if way == 0 else ((ny - step) % ny, ny - 1 - step)
        return src, dst, which

    ag = []
    for way in range(2):
        ag.append([])
        for i in range(ny - 1):
            src, dst, which = ag_place(way, i)
            chunk = pl.ds(which * quarter, quarter)
            ag[way].append(
                remote(ring.at[src, chunk], ring.at[dst, chunk], ag_send.at[way, i], ag_recv.at[way, i], (right, left)[way])
            )
    for i in range(2):
        for way in range(2):
            ag[way][i].start()
    copy_ws = remote(
        down_hbm.at[:, 1 - core],
        wext.at[:, pl.ds(pad, cols), pl.ds(feat, feat)],
        sib_send.at[0],
        sib_recv.at[0],
        other,
    )
    copy_ws.start()

    copy_r.wait()
    copy_k.wait()
    copy_o.wait()
    with jax.named_scope("routing"):
        named = jnp.zeros((ne, tok), F32)
        gate = jnp.zeros((ne, tok), F32)
        for k in range(top):
            hit = routes_ref[k : k + 1, :] == iota((ne, tok), 0)
            named = named + jnp.where(hit, 1.0, 0.0)
            gate = gate + jnp.where(hit, gates_ref[k : k + 1, :], 0.0)
        earlier = jnp.where(iota((tok, tok), 0) < iota((tok, tok), 1), 1.0, 0.0).astype(BF)
        slot = jnp.where(named > 0.5, dot(named.astype(BF), earlier), 100.0)
        gate_1 = gate.astype(BF)
        gate_2 = (gate - gate_1.astype(F32)).astype(BF)
        gate_3 = (gate - gate_1.astype(F32) - gate_2.astype(F32)).astype(BF)

        spread = jnp.where(iota((span, ne), 0) // GROUP == iota((span, ne), 1), 1.0, 0.0).astype(BF)
        place = (iota((span, tok), 0) % GROUP).astype(F32)
        takes = dot(spread, slot.astype(BF)) == place
        gate_rows = dot(spread, gate_1) + dot(spread, gate_2) + dot(spread, gate_3)
        gate_rows = jnp.sum(jnp.where(takes, gate_rows, 0.0), axis=1, keepdims=True)
        takes = jnp.where(takes, 1.0, 0.0).astype(BF)
        send_g[...] = (dot(takes, grad_ref[...]) * gate_rows).astype(BF)

    def group(e):
        return pl.ds(pl.multiple_of(e * GROUP, GROUP), GROUP)

    def exchange(src, dst, n, low, count, stride):
        def one(i, carry):
            peer = low + (me + i * stride) % count

            @pl.when(peer != me)
            def _():
                pltpu.make_async_remote_copy(
                    src_ref=src.at[group(peer)],
                    dst_ref=dst.at[group(me)],
                    send_sem=a2a_send.at[n],
                    recv_sem=a2a_recv.at[n],
                    device_id=(peer, tt),
                    device_id_type=MESH,
                ).start()

            return carry

        lax.fori_loop(0, count, one, 0)

    def exchanged(src, dst, n):
        all_but_one = pl.ds(0, span - GROUP)
        return remote(src.at[all_but_one], dst.at[all_but_one], a2a_send.at[n], a2a_recv.at[n], other)

    exchange(send_g, recv_g, 0, 0, ne, STRIDE)
    recv_g[group(me), :] = send_g[group(me), :]

    packed, padded = GROUP * cap, GROUP * GROUP

    def selection(row, col):
        return jnp.where((row == cap * (col // GROUP) + col % GROUP) & (col % GROUP < cap), 1.0, 0.0).astype(BF)

    compact = selection(iota((packed, padded), 0), iota((packed, padded), 1))
    expand = selection(iota((padded, packed), 1), iota((padded, packed), 0))

    copy_w.wait()
    copy_ws.wait_recv()

    def forward(d, g, first):
        weights = wext.at[(y + ny - d) % ny]
        for side, lanes, depth in ((0, slice(0, 256), slice(pad, pad + 256)), (1, slice(wide - 256, wide), slice(0, 256))):
            out = slice((2 * g + side) * quarter, (2 * g + side + 1) * quarter)
            block = ring[d, g * quarter : (g + 1) * quarter, lanes]
            own = dot(block, weights[depth, 0:feat])
            sib = dot(block, weights[depth, feat:])
            acc_own[out, :] = own if first else acc_own[out, :] + own
            acc_sib[out, :] = sib if first else acc_sib[out, :] + sib

    def ag_hop(i):
        for way in range(2):
            ag[way][i].wait_recv()
            if i + 2 < ny - 1:
                ag[way][i + 2].start()
        for way in range(2):
            _, dst, which = ag_place(way, i)
            forward(dst, which, False)

    copy_e = []
    for g in range(2):
        block = pl.ds(g * half, half)
        copy_e.append(remote(acc_sib.at[block], sib_in.at[block], sib_send.at[2 + g], sib_recv.at[2 + g], other))

    def give_back(g):
        copy_e[g].wait_recv()
        per = ne // GROUP // 2
        for b in range(g * per, (g + 1) * per):
            block = slice(b * packed, (b + 1) * packed)
            total = (acc_own[block, :] + sib_in[block, :]).astype(BF)
            send_e[b * padded : (b + 1) * padded, :] = dot(expand, total).astype(BF)
        exchange(send_e, recv_e, 1, g * (ne // 2), ne // 2, HALF_STRIDE)

        @pl.when(me // (ne // 2) == g)
        def _():
            recv_e[group(me), :] = send_e[group(me), :]

    forward(0, 0, True)
    forward(0, 1, True)
    for i in range(ny - 3):
        ag_hop(i)
    exchanged(send_g, recv_g, 0).wait_recv()
    for b in range(ne // GROUP):
        rg[b * packed : (b + 1) * packed, 0:feat] = dot(compact, recv_g[b * padded : (b + 1) * padded, :]).astype(BF)
    copy_rg = remote(rg.at[:, pl.ds(0, feat)], rg.at[:, pl.ds(feat, feat)], sib_send.at[1], sib_recv.at[1], other)
    copy_rg.start()

    for i in range(ny - 3, ny - 1):
        ag_hop(i)
    for copy in copy_e:
        copy.start()

    def backward(d):
        weights = wext.at[(y + d) % ny]
        for g in range(2):
            out = slice(g * quarter, (g + 1) * quarter)
            low = dot_nt(rg[2 * g * quarter : (2 * g + 1) * quarter, :], weights[pad : pad + 256, :])
            high = dot_nt(rg[(2 * g + 1) * quarter : (2 * g + 2) * quarter, :], weights[0:256, :])
            part[d, out, 0:128] = low[:, 0:128]
            part[d, out, 128:256] = low[:, 128:256] + high[:, 0:128]
            part[d, out, 256:384] = high[:, 128:256]

    far = ny // 2
    rs_place, rs = [], []
    for way in range(2):
        places = [(far, 0, way), (far, 1, way)]
        for step in range(1, far + 1):
            d = (far - step if way == 0 else far + step) % ny
            places += [(d, 0, 1 - way), (d, 1, 1 - way), (d, 0, way), (d, 1, way)]
        rs_place.append(places)
        rs.append({})
        for i, (d, g, which) in enumerate(places):
            if d:
                chunk = pl.ds(0, subs[which][1])
                rs[way][d, g, which] = (
                    i,
                    remote(
                        rs_out.at[way, i, chunk], rs_in.at[way, i, chunk],
                        rs_send.at[way, i], rs_recv.at[way, i], (right, left)[way],
                    ),
                )

    def rs_share(d, g, which):
        first, size = subs[which]
        return part[d, g * quarter + first : g * quarter + first + size, :]

    def rs_arrived(way, d, g, which):
        before = ((d + 1) if way == 0 else (d + ny - 1) % ny, g, which)
        if before not in rs[way]:
            return None
        i, copy = rs[way][before]
        copy.wait_recv()
        return rs_in[way, i, 0 : subs[which][1], :].astype(F32)

    def rs_step(way, n):
        d, g, which = rs_place[way][n]
        arrived = rs_arrived(way, d, g, which)
        total = rs_share(d, g, which)
        if arrived is not None:
            total = total + arrived
        i, copy = rs[way][d, g, which]
        rs_out[way, i, 0 : subs[which][1], :] = total.astype(BF)
        copy.start()

    copy_rg.wait_recv()
    backward(far)
    for n in range(2):
        for way in range(2):
            rs_step(way, n)
    backward(far - 1)
    for n in range(2, 4):
        rs_step(0, n)
    backward(far + 1)
    for n in range(2, 4):
        rs_step(1, n)
    give_back(0)
    give_back(1)
    backward(far - 2)
    backward(far + 2)

    done = {far, far - 1, far + 1, far - 2, far + 2}
    def rs_both(n):
        for way in range(2):
            d = rs_place[way][n][0]
            if d not in done:
                backward(d)
                done.add(d)
            rs_step(way, n)

    for n in range(4, 4 * far - 2):
        rs_both(n)
    backward(0)

    with jax.named_scope("combine"):
        slot_t = jnp.transpose(slot).astype(BF)
        gate_t = jnp.transpose(gate)
        gate_1 = gate_t.astype(BF)
        gate_2 = (gate_t - gate_1.astype(F32)).astype(BF)
        gate_3 = (gate_t - gate_1.astype(F32) - gate_2.astype(F32)).astype(BF)
        spread_t = jnp.where(iota((ne, span), 1) // GROUP == iota((ne, span), 0), 1.0, 0.0).astype(BF)
        place_t = (iota((tok, span), 1) % GROUP).astype(F32)
        takes_t = dot(slot_t, spread_t) == place_t
        mixing = [jnp.where(takes_t, dot(g, spread_t), 0.0).astype(BF) for g in (gate_1, gate_2, gate_3)]
        exchanged(send_e, recv_e, 1).wait_recv()
        mixed_ref[...] = (
            dot(mixing[0], recv_e[...]) + dot(mixing[1], recv_e[...]) + dot(mixing[2], recv_e[...])
        ).astype(BF)

    last = {}
    for n in range(4 * far - 2, 4 * far + 2):
        for way in range(2):
            _, g, which = rs_place[way][n]
            if (g, which) not in last:
                last[g, which] = rs_share(0, g, which)
            last[g, which] = last[g, which] + rs_arrived(way, 0, g, which)
    for (g, which), total in last.items():
        first, size = subs[which]
        total = total.astype(BF)
        for side in range(2):
            at = (2 * g + side) * quarter + first
            hgrad_ref[at : at + size, :] = total[:, side * cols : (side + 1) * cols]

    for way in range(2):
        for copy in ag[way]:
            copy.wait_send()
        for _, copy in rs[way].values():
            copy.wait_send()
    for copy in (copy_ws, copy_rg, copy_e[0], copy_e[1]):
        copy.wait_send()
    exchanged(send_g, recv_g, 0).wait_send()
    exchanged(send_e, recv_e, 1).wait_send()


def body(routes, gates, hidden, down, out_grad):
    ne, nt = lax.axis_size("expert"), lax.axis_size("tensor")
    ny = nt // 2
    tok, top = routes.shape
    rows, cols = hidden.shape[1:]
    feat = out_grad.shape[1]
    cap = rows // ne
    sizes = (ne, ny, cap, tok, top, rows, cols, feat)
    half, wide = rows // 2, 2 * cols
    sub = (rows // 8 + 15) // 16 * 16
    span = ne * GROUP
    vmem, hbm = pl.BlockSpec(memory_space=pltpu.VMEM), pl.BlockSpec(memory_space=pltpu.HBM)
    dma = pltpu.SemaphoreType.DMA
    mixed, hgrad = pl.pallas_call(
        functools.partial(kernel, sizes),
        out_shape=(
            jax.ShapeDtypeStruct((tok, feat), BF),
            jax.ShapeDtypeStruct((rows, cols), BF),
        ),
        in_specs=[hbm] * 5,
        out_specs=(vmem, vmem),
        scratch_shapes=[
            pltpu.VMEM((top, tok), jnp.int32),
            pltpu.VMEM((top, tok), F32),
            pltpu.VMEM((tok, feat), BF),
            pltpu.VMEM((cols, rows), BF),
            pltpu.VMEM((ny, 512 - cols, 2 * feat), BF),
            pltpu.VMEM((ny, half, wide), BF),
            pltpu.VMEM((rows, feat), F32),
            pltpu.VMEM((rows, feat), F32),
            pltpu.VMEM((rows, feat), F32),
            pltpu.VMEM((rows, 2 * feat), BF),
            pltpu.VMEM((ny, half, wide), F32),
            pltpu.VMEM((2, 2 * ny - 2, sub, wide), BF),
            pltpu.VMEM((2, 2 * ny - 2, sub, wide), BF),
            pltpu.VMEM((span, feat), BF),
            pltpu.VMEM((span, feat), BF),
            pltpu.VMEM((span, feat), BF),
            pltpu.VMEM((span, feat), BF),
            dma((5,)),
            dma((2, ny - 1)),
            dma((2, ny - 1)),
            dma((2, 2 * ny - 2)),
            dma((2, 2 * ny - 2)),
            dma((4,)),
            dma((4,)),
            dma((2,)),
            dma((2,)),
        ],
        compiler_params=pltpu.CompilerParams(
            collective_id=0, has_side_effects=True, vmem_limit_bytes=48 * 1024 * 1024
        ),
    )(*[pltpu.with_memory_space_constraint(a, pltpu.HBM) for a in (routes.T, gates.T, out_grad, hidden[0].T, down.reshape(ny, 2, cols, feat))])
    return mixed, hgrad[None]


def solution(mesh):
    return jax.shard_map(
        body,
        mesh=mesh,
        in_specs=(
            P("expert", None),
            P("expert", None),
            P("expert", None, "tensor"),
            P("expert", None, "tensor"),
            P("expert", "tensor"),
        ),
        out_specs=(P("expert", "tensor"), P("expert", None, "tensor")),
        check_vma=False,
    )
```

```python
import functools

import jax
import jax.numpy as jnp
from jax import lax
from jax.experimental import pallas as pl
from jax.experimental.pallas import tpu as pltpu
from jax.sharding import PartitionSpec as P

MESH = pl.DeviceIdType.MESH
GROUP = 48
STRIDE = 11
BF, F32 = jnp.bfloat16, jnp.float32


def dot(a, b):
    return jnp.dot(a, b, preferred_element_type=F32)


def dot_nt(a, b):
    return lax.dot_general(a, b, (((1,), (1,)), ((), ())), preferred_element_type=F32)


def iota(shape, axis):
    return lax.broadcasted_iota(jnp.int32, shape, axis)


def lane_groups(count, width):
    lane = iota((1, count * width), 1)
    group = jnp.zeros((1, count * width), jnp.int32)
    for m in range(1, count):
        group = group + jnp.where(lane >= m * width, 1, 0)
    return group, lane - group * width


def kernel(
    sizes,
    routes_hbm, gates_hbm, grad_hbm, hidden_hbm, down_hbm,
    mixed_ref, hgrad_ref,
    routes_ref, gates_ref, grads, hin, wext, ring, acc, sib_in, rg,
    part, rs_out, rs_in, send_g, recv_g, send_e, recv_e, mix_part, mix_in,
    local_sem, ag_send, ag_recv, rs_send, rs_recv, sib_send, sib_recv, a2a_send, a2a_recv,
):
    ne, ny, cap, tok, top, rows, cols, feat = sizes
    half, quarter = rows // 2, rows // 4
    wide = 2 * cols
    pad = 256 - cols
    peers = ne // 2
    span = peers * GROUP
    tiles = 2 * feat // 128
    cut = (quarter // 2 + 15) // 16 * 16
    subs = ((0, cut), (cut, quarter - cut))
    me = lax.axis_index("expert")
    tt = lax.axis_index("tensor")
    y, core = tt // 2, tt % 2
    right = ((y + 1) % ny) * 2 + core
    left = ((y + ny - 1) % ny) * 2 + core
    other = y * 2 + (1 - core)
    reach = (me // peers + core) % 2
    rows_at = pl.multiple_of(reach * half, 16)
    rows_other = pl.multiple_of((1 - reach) * half, 16)
    own_feat = pl.multiple_of(core * feat, 128)

    copy_h = pltpu.make_async_copy(hidden_hbm, hin, local_sem.at[0])
    copy_r = pltpu.make_async_copy(routes_hbm, routes_ref, local_sem.at[1])
    copy_k = pltpu.make_async_copy(gates_hbm, gates_ref, local_sem.at[2])
    copy_w = pltpu.make_async_copy(
        down_hbm.at[:, core], wext.at[:, pl.ds(pad, cols), pl.ds(own_feat, feat)], local_sem.at[3]
    )
    grad_tiles = []
    for i in range(feat // 128):
        at = pl.multiple_of((core * (feat // 128) + i) * tok, 16)
        grad_tiles.append((grad_hbm.at[:, pl.ds(i * 128, 128)], grads.at[pl.ds(at, tok)]))
    copy_o = [pltpu.make_async_copy(src, dst, local_sem.at[4 + i]) for i, (src, dst) in enumerate(grad_tiles)]
    for copy in (copy_h, copy_r, copy_k, *copy_o, copy_w):
        copy.start()

    barrier = pltpu.get_barrier_semaphore()

    def greet(i, carry):
        peer = reach * peers + (me + i) % peers

        @pl.when(peer != me)
        def _():
            pl.semaphore_signal(barrier, inc=1, device_id=(peer, tt), device_id_type=MESH)

        return carry

    for peer in (right, left, other):
        pl.semaphore_signal(barrier, inc=1, device_id=(me, peer), device_id_type=MESH)
    lax.fori_loop(0, peers, greet, 0, unroll=8)

    wext[:, 0:pad, :] = jnp.zeros((ny, pad, 2 * feat), BF)
    wext[:, pad + cols :, :] = jnp.zeros((ny, pad, 2 * feat), BF)

    copy_h.wait()
    own_rows = jnp.transpose(hin[...])
    for q in range(4):
        g, side = q // 2, q % 2
        ring[0, g * quarter : (g + 1) * quarter, side * cols : (side + 1) * cols] = own_rows[q * quarter : (q + 1) * quarter, :]

    pl.semaphore_wait(barrier, peers - 1 + core + 3)

    def remote(src, dst, send, recv, peer):
        return pltpu.make_async_remote_copy(
            src_ref=src, dst_ref=dst, send_sem=send, recv_sem=recv, device_id=(me, peer), device_id_type=MESH
        )

    def ag_place(way, i):
        step, which = i // 2, (i % 2) ^ way
        src, dst = (step, step + 1) if way == 0 else ((ny - step) % ny, ny - 1 - step)
        return src, dst, which

    ag = []
    for way in range(2):
        ag.append([])
        for i in range(ny - 1):
            src, dst, which = ag_place(way, i)
            chunk = pl.ds(which * quarter, quarter)
            ag[way].append(
                remote(ring.at[src, chunk], ring.at[dst, chunk], ag_send.at[way, i], ag_recv.at[way, i], (right, left)[way])
            )
    for i in range(2):
        for way in range(2):
            ag[way][i].start()
    copy_os = [remote(src, dst, sib_send.at[3 + i], sib_recv.at[3 + i], other) for i, (src, dst) in enumerate(grad_tiles)]
    for copy in copy_os:
        copy.start()
    copy_ws = remote(
        down_hbm.at[:, 1 - core],
        wext.at[:, pl.ds(pad, cols), pl.ds(own_feat, feat)],
        sib_send.at[0],
        sib_recv.at[0],
        other,
    )
    copy_ws.start()

    copy_r.wait()
    copy_k.wait()
    with jax.named_scope("routing"):
        named = jnp.zeros((ne, tok), F32)
        gate = jnp.zeros((ne, tok), F32)
        for k in range(top):
            hit = routes_ref[k : k + 1, :] == iota((ne, tok), 0)
            named = named + jnp.where(hit, 1.0, 0.0)
            gate = gate + jnp.where(hit, gates_ref[k : k + 1, :], 0.0)
        earlier = jnp.where(iota((tok, tok), 0) < iota((tok, tok), 1), 1.0, 0.0).astype(BF)
        slot = jnp.where(named > 0.5, dot(named.astype(BF), earlier), 100.0)
        token, lane = iota((tok, tiles * tok), 0), iota((tok, tiles * tok), 1)
        repeat = jnp.zeros((tok, tiles * tok), F32)
        offset = jnp.zeros((1, tiles * tok), F32)
        for j in range(tiles):
            repeat = repeat + jnp.where(lane == token + j * tok, 1.0, 0.0)
            offset = offset + jnp.where(lane[0:1, :] >= (j + 1) * tok, float(cap), 0.0)
        repeat = repeat.astype(BF)

        def thirds(x):
            first = x.astype(BF)
            second = (x - first.astype(F32)).astype(BF)
            return first, second, (x - first.astype(F32) - second.astype(F32)).astype(BF)

        slot_4 = dot(slot.astype(BF), repeat) + offset
        gate_4 = sum(dot(g, repeat) for g in thirds(gate))
        spread = iota((peers, GROUP, ne), 2) == iota((peers, GROUP, ne), 0) + reach * peers
        spread = jnp.where(spread, 1.0, 0.0).reshape(span, ne).astype(BF)
        place = iota((peers, GROUP, tiles * tok), 1).reshape(span, tiles * tok).astype(F32)
        takes = dot(spread, slot_4.astype(BF)) == place
        gate_rows = sum(dot(spread, g) for g in thirds(gate_4))
        gate_rows = jnp.sum(jnp.where(takes, gate_rows, 0.0), axis=1, keepdims=True)
        takes = jnp.where(takes, 1.0, 0.0).astype(BF)
        for copy in copy_o:
            copy.wait()
        for copy in copy_os:
            copy.wait_recv()
        send_g[...] = (dot(takes, grads[...]) * gate_rows).astype(BF)

    def group(u):
        return pl.ds(pl.multiple_of(u * GROUP, 16), GROUP)

    own_group = group(me % peers)

    def exchange(src, dst, n):
        def one(i, carry):
            u = (me + i * STRIDE) % peers
            peer = reach * peers + u

            @pl.when(peer != me)
            def _():
                pltpu.make_async_remote_copy(
                    src_ref=src.at[group(u)],
                    dst_ref=dst.at[own_group],
                    send_sem=a2a_send.at[n],
                    recv_sem=a2a_recv.at[n],
                    device_id=(peer, tt),
                    device_id_type=MESH,
                ).start()

            return carry

        lax.fori_loop(0, peers, one, 0)

        @pl.when(core == 0)
        def _():
            dst[own_group, :] = src[own_group, :]

    def exchanged(src, dst, n, wait):
        for c in range(2):

            @pl.when(core == c)
            def _(c=c):
                every = pl.ds(0, span - (1 - c) * GROUP)
                getattr(remote(src.at[every], dst.at[every], a2a_send.at[n], a2a_recv.at[n], other), wait)()

    exchange(send_g, recv_g, 0)

    packed, padded = 16 * cap, 16 * GROUP
    pair, row = lane_groups(16, GROUP)
    compact, expand = [], []
    for j in range(tiles):
        at = row - j * cap
        named_row = jnp.where((at >= 0) & (at < cap), pair * cap + at, -1)
        compact.append(jnp.where(iota((packed, padded), 0) == named_row, 1.0, 0.0).astype(BF))
        at = iota((16, GROUP, packed), 1) - j * cap
        hit = (iota((16, GROUP, packed), 2) == iota((16, GROUP, packed), 0) * cap + at) & (at >= 0) & (at < cap)
        expand.append(jnp.where(hit, 1.0, 0.0).reshape(padded, packed).astype(BF))

    copy_w.wait()
    copy_ws.wait_recv()

    def forward(d, g, first):
        weights = wext.at[(y + ny - d) % ny]
        for side, lanes, depth in ((0, slice(0, 256), slice(pad, pad + 256)), (1, slice(wide - 256, wide), slice(0, 256))):
            out = slice((2 * g + side) * quarter, (2 * g + side + 1) * quarter)
            block = ring[d, g * quarter : (g + 1) * quarter, lanes]
            share = dot(block, weights[depth, :])
            acc[out, :] = share if first else acc[out, :] + share

    def ag_hop(i):
        for way in range(2):
            ag[way][i].wait_recv()
            if i + 2 < ny - 1:
                ag[way][i + 2].start()
        for way in range(2):
            _, dst, which = ag_place(way, i)
            forward(dst, which, False)

    copy_e = remote(acc.at[pl.ds(rows_other, half)], sib_in, sib_send.at[2], sib_recv.at[2], other)

    def give_back():
        copy_e.wait_recv()
        for b in range(peers // 16):
            total = (acc[pl.ds(rows_at + b * packed, packed), :] + sib_in[b * packed : (b + 1) * packed, :]).astype(BF)
            out = sum(dot(expand[j], total[:, j * 128 : (j + 1) * 128]) for j in range(tiles))
            send_e[b * padded : (b + 1) * padded, :] = out.astype(BF)
        exchange(send_e, recv_e, 1)

    forward(0, 0, True)
    forward(0, 1, True)
    for i in range(ny - 5):
        ag_hop(i)
    ag_hop(3)
    ag_hop(4)
    exchanged(send_g, recv_g, 0, "wait_recv")
    for b in range(peers // 16):
        arrived = recv_g[b * padded : (b + 1) * padded, :]
        for j in range(tiles):
            rg[pl.ds(rows_at + b * packed, packed), j * 128 : (j + 1) * 128] = dot(compact[j], arrived).astype(BF)
    rg_half = rg.at[pl.ds(rows_at, half)]
    copy_rg = remote(rg_half, rg_half, sib_send.at[1], sib_recv.at[1], other)
    copy_rg.start()

    ag_hop(5)
    def backward(d):
        weights = wext.at[(y + d) % ny]
        for g in range(2):
            out = slice(g * quarter, (g + 1) * quarter)
            low = dot_nt(rg[2 * g * quarter : (2 * g + 1) * quarter, :], weights[pad : pad + 256, :])
            high = dot_nt(rg[(2 * g + 1) * quarter : (2 * g + 2) * quarter, :], weights[0:256, :])
            part[d, out, 0:128] = low[:, 0:128]
            part[d, out, 128:256] = low[:, 128:256] + high[:, 0:128]
            part[d, out, 256:384] = high[:, 128:256]

    far = ny // 2
    rs_place, rs = [], []
    for way in range(2):
        places = [(far, 0, way), (far, 1, way)]
        for step in range(1, far + 1):
            d = (far - step if way == 0 else far + step) % ny
            places += [(d, 0, 1 - way), (d, 1, 1 - way), (d, 0, way), (d, 1, way)]
        rs_place.append(places)
        rs.append({})
        for i, (d, g, which) in enumerate(places):
            if d:
                chunk = pl.ds(0, subs[which][1])
                rs[way][d, g, which] = (
                    i,
                    remote(
                        rs_out.at[way, i, chunk], rs_in.at[way, i, chunk],
                        rs_send.at[way, i], rs_recv.at[way, i], (right, left)[way],
                    ),
                )

    def rs_share(d, g, which):
        first, size = subs[which]
        return part[d, g * quarter + first : g * quarter + first + size, :]

    def rs_arrived(way, d, g, which):
        before = ((d + 1) if way == 0 else (d + ny - 1) % ny, g, which)
        if before not in rs[way]:
            return None
        i, copy = rs[way][before]
        copy.wait_recv()
        return rs_in[way, i, 0 : subs[which][1], :].astype(F32)

    def rs_step(way, n):
        d, g, which = rs_place[way][n]
        arrived = rs_arrived(way, d, g, which)
        total = rs_share(d, g, which)
        if arrived is not None:
            total = total + arrived
        i, copy = rs[way][d, g, which]
        rs_out[way, i, 0 : subs[which][1], :] = total.astype(BF)
        copy.start()

    copy_rg.wait_recv()
    backward(far)
    for n in range(2):
        for way in range(2):
            rs_step(way, n)
    backward(far - 1)
    for n in range(2, 4):
        rs_step(0, n)
    backward(far + 1)
    for n in range(2, 4):
        rs_step(1, n)
    ag_hop(6)
    copy_e.start()
    backward(far - 2)
    backward(far + 2)
    give_back()

    done = {far, far - 1, far + 1, far - 2, far + 2}
    def rs_both(n):
        for way in range(2):
            d = rs_place[way][n][0]
            if d not in done:
                backward(d)
                done.add(d)
            rs_step(way, n)

    for n in range(4, 4 * far - 2):
        rs_both(n)
    backward(0)

    with jax.named_scope("combine"):
        pair, row = lane_groups(peers, GROUP)
        spread_t = jnp.where(iota((ne, span), 0) == pair + reach * peers, 1.0, 0.0).astype(BF)
        takes_t = dot(jnp.transpose(slot_4).astype(BF), spread_t) == row.astype(F32)
        mixing = [jnp.where(takes_t, dot(g, spread_t), 0.0).astype(BF) for g in thirds(jnp.transpose(gate_4))]
    exchanged(send_e, recv_e, 1, "wait_recv")
    arrived = recv_e[...]
    mix_part[...] = dot(mixing[0], arrived) + dot(mixing[1], arrived) + dot(mixing[2], arrived)
    mix_rows = tiles // 2 * tok
    copy_m = remote(
        mix_part.at[pl.ds(pl.multiple_of((1 - core) * mix_rows, 16), mix_rows)], mix_in, sib_send.at[5], sib_recv.at[5], other
    )
    copy_m.start()

    last = {}
    for n in range(4 * far - 2, 4 * far + 2):
        for way in range(2):
            _, g, which = rs_place[way][n]
            if (g, which) not in last:
                last[g, which] = rs_share(0, g, which)
            last[g, which] = last[g, which] + rs_arrived(way, 0, g, which)
    for (g, which), total in last.items():
        first, size = subs[which]
        total = total.astype(BF)
        for side in range(2):
            at = (2 * g + side) * quarter + first
            hgrad_ref[at : at + size, :] = total[:, side * cols : (side + 1) * cols]

    copy_m.wait_recv()
    mixed = (mix_part[pl.ds(pl.multiple_of(core * mix_rows, 16), mix_rows), :] + mix_in[...]).astype(BF)
    for i in range(tiles // 2):
        mixed_ref[:, i * 128 : (i + 1) * 128] = mixed[i * tok : (i + 1) * tok, :]

    for way in range(2):
        for copy in ag[way]:
            copy.wait_send()
        for _, copy in rs[way].values():
            copy.wait_send()
    for copy in (copy_ws, copy_rg, copy_e, copy_m, *copy_os):
        copy.wait_send()
    exchanged(send_g, recv_g, 0, "wait_send")
    exchanged(send_e, recv_e, 1, "wait_send")


def body(routes, gates, hidden, down, out_grad):
    ne, nt = lax.axis_size("expert"), lax.axis_size("tensor")
    ny = nt // 2
    tok, top = routes.shape
    rows, cols = hidden.shape[1:]
    feat = out_grad.shape[1]
    cap = rows // ne
    sizes = (ne, ny, cap, tok, top, rows, cols, feat)
    half, wide = rows // 2, 2 * cols
    sub = (rows // 8 + 15) // 16 * 16
    span = ne // 2 * GROUP
    vmem, hbm = pl.BlockSpec(memory_space=pltpu.VMEM), pl.BlockSpec(memory_space=pltpu.HBM)
    dma = pltpu.SemaphoreType.DMA
    mixed, hgrad = pl.pallas_call(
        functools.partial(kernel, sizes),
        out_shape=(
            jax.ShapeDtypeStruct((tok, feat), BF),
            jax.ShapeDtypeStruct((rows, cols), BF),
        ),
        in_specs=[hbm] * 5,
        out_specs=(vmem, vmem),
        scratch_shapes=[
            pltpu.VMEM((top, tok), jnp.int32),
            pltpu.VMEM((top, tok), F32),
            pltpu.VMEM((feat // 64 * tok, 128), BF),
            pltpu.VMEM((cols, rows), BF),
            pltpu.VMEM((ny, 512 - cols, 2 * feat), BF),
            pltpu.VMEM((ny, half, wide), BF),
            pltpu.VMEM((rows, 2 * feat), F32),
            pltpu.VMEM((half, 2 * feat), F32),
            pltpu.VMEM((rows, 2 * feat), BF),
            pltpu.VMEM((ny, half, wide), F32),
            pltpu.VMEM((2, 2 * ny - 2, sub, wide), BF),
            pltpu.VMEM((2, 2 * ny - 2, sub, wide), BF),
            pltpu.VMEM((span, 128), BF),
            pltpu.VMEM((span, 128), BF),
            pltpu.VMEM((span, 128), BF),
            pltpu.VMEM((span, 128), BF),
            pltpu.VMEM((feat // 64 * tok, 128), F32),
            pltpu.VMEM((feat // 128 * tok, 128), F32),
            dma((4 + feat // 128,)),
            dma((2, ny - 1)),
            dma((2, ny - 1)),
            dma((2, 2 * ny - 2)),
            dma((2, 2 * ny - 2)),
            dma((6,)),
            dma((6,)),
            dma((2,)),
            dma((2,)),
        ],
        compiler_params=pltpu.CompilerParams(
            collective_id=0, has_side_effects=True, vmem_limit_bytes=48 * 1024 * 1024
        ),
    )(*[pltpu.with_memory_space_constraint(a, pltpu.HBM) for a in (routes.T, gates.T, out_grad, hidden[0].T, down.reshape(ny, 2, cols, feat))])
    return mixed, hgrad[None]


def solution(mesh):
    return jax.shard_map(
        body,
        mesh=mesh,
        in_specs=(
            P("expert", None),
            P("expert", None),
            P("expert", None, "tensor"),
            P("expert", None, "tensor"),
            P("expert", "tensor"),
        ),
        out_specs=(P("expert", "tensor"), P("expert", None, "tensor")),
        check_vma=False,
    )
```

```python
import functools

import jax
import jax.numpy as jnp
from jax import lax
from jax.experimental import pallas as pl
from jax.experimental.pallas import tpu as pltpu
from jax.sharding import PartitionSpec as P

MESH = pl.DeviceIdType.MESH
GROUP = 48
STRIDE = 11
BF, F32 = jnp.bfloat16, jnp.float32


def dot(a, b):
    return jnp.dot(a, b, preferred_element_type=F32)


def dot_nt(a, b):
    return lax.dot_general(a, b, (((1,), (1,)), ((), ())), preferred_element_type=F32)


def iota(shape, axis):
    return lax.broadcasted_iota(jnp.int32, shape, axis)


def lane_groups(count, width):
    lane = iota((1, count * width), 1)
    group = jnp.zeros((1, count * width), jnp.int32)
    for m in range(1, count):
        group = group + jnp.where(lane >= m * width, 1, 0)
    return group, lane - group * width


def kernel(
    sizes,
    routes_hbm, gates_hbm, grad_hbm, hidden_hbm, down_hbm,
    mixed_ref, hgrad_ref,
    routes_ref, gates_ref, grads, hin, wext, ring, acc, sib_in, rg,
    part, rs_out, rs_in, send_g, recv_g, send_e, recv_e, mix_part, mix_in,
    ready_sem, local_sem, ag_send, ag_recv, rs_send, rs_recv, sib_send, sib_recv, a2a_send, a2a_recv,
):
    ne, ny, cap, tok, top, rows, cols, feat = sizes
    half, quarter = rows // 2, rows // 4
    wide = 2 * cols
    pad = 256 - cols
    peers = ne // 2
    span = peers * GROUP
    tiles = 2 * feat // 128
    cut = (quarter // 2 + 15) // 16 * 16
    subs = ((0, cut), (cut, quarter - cut))
    me = lax.axis_index("expert")
    tt = lax.axis_index("tensor")
    y, core = tt // 2, tt % 2
    right = ((y + 1) % ny) * 2 + core
    left = ((y + ny - 1) % ny) * 2 + core
    other = y * 2 + (1 - core)
    reach = (me // peers + core) % 2
    rows_at = pl.multiple_of(reach * half, 16)
    rows_other = pl.multiple_of((1 - reach) * half, 16)
    own_feat = pl.multiple_of(core * feat, 128)

    copy_h = pltpu.make_async_copy(hidden_hbm, hin, local_sem.at[0])
    copy_r = pltpu.make_async_copy(routes_hbm, routes_ref, local_sem.at[1])
    copy_k = pltpu.make_async_copy(gates_hbm, gates_ref, local_sem.at[2])
    copy_w = pltpu.make_async_copy(
        down_hbm.at[:, core], wext.at[:, pl.ds(pad, cols), pl.ds(own_feat, feat)], local_sem.at[3]
    )
    grad_tiles = []
    for i in range(feat // 128):
        at = pl.multiple_of((core * (feat // 128) + i) * tok, 16)
        grad_tiles.append((grad_hbm.at[:, pl.ds(i * 128, 128)], grads.at[pl.ds(at, tok)]))
    copy_o = [pltpu.make_async_copy(src, dst, local_sem.at[4 + i]) for i, (src, dst) in enumerate(grad_tiles)]
    for copy in (copy_h, copy_r, copy_k, *copy_o, copy_w):
        copy.start()

    barrier = pltpu.get_barrier_semaphore()

    def greet(i, carry):
        peer = reach * peers + (me + i) % peers

        @pl.when(peer != me)
        def _():
            pl.semaphore_signal(barrier, inc=1, device_id=(peer, tt), device_id_type=MESH)

        return carry

    for chip in (right, left):
        pl.semaphore_signal(barrier, inc=1, device_id=(me, chip // 2 * 2), device_id_type=MESH)

    @pl.when(core == 1)
    def _():
        pl.semaphore_signal(barrier, inc=1, device_id=(me, other), device_id_type=MESH)

    lax.fori_loop(0, peers, greet, 0, unroll=8)

    wext[:, 0:pad, :] = jnp.zeros((ny, pad, 2 * feat), BF)
    wext[:, pad + cols :, :] = jnp.zeros((ny, pad, 2 * feat), BF)

    copy_h.wait()
    own_rows = jnp.transpose(hin[...])
    for q in range(4):
        g, side = q // 2, q % 2
        ring[0, g * quarter : (g + 1) * quarter, side * cols : (side + 1) * cols] = own_rows[q * quarter : (q + 1) * quarter, :]

    @pl.when(core == 0)
    def _():
        pl.semaphore_wait(barrier, peers - 1 + 5)
        pl.semaphore_signal(ready_sem, inc=1, device_id=(me, other), device_id_type=MESH)

    @pl.when(core == 1)
    def _():
        pl.semaphore_wait(ready_sem, 1)


    def remote(src, dst, send, recv, peer):
        return pltpu.make_async_remote_copy(
            src_ref=src, dst_ref=dst, send_sem=send, recv_sem=recv, device_id=(me, peer), device_id_type=MESH
        )

    def ag_place(way, i):
        step, which = i // 2, (i % 2) ^ way
        src, dst = (step, step + 1) if way == 0 else ((ny - step) % ny, ny - 1 - step)
        return src, dst, which

    ag = []
    for way in range(2):
        ag.append([])
        for i in range(ny - 1):
            src, dst, which = ag_place(way, i)
            chunk = pl.ds(which * quarter, quarter)
            ag[way].append(
                remote(ring.at[src, chunk], ring.at[dst, chunk], ag_send.at[way, i], ag_recv.at[way, i], (right, left)[way])
            )
    for i in range(2):
        for way in range(2):
            ag[way][i].start()
    copy_os = [remote(src, dst, sib_send.at[3 + i], sib_recv.at[3 + i], other) for i, (src, dst) in enumerate(grad_tiles)]
    for copy in copy_os:
        copy.start()
    copy_ws = remote(
        down_hbm.at[:, 1 - core],
        wext.at[:, pl.ds(pad, cols), pl.ds(own_feat, feat)],
        sib_send.at[0],
        sib_recv.at[0],
        other,
    )
    copy_ws.start()

    copy_r.wait()
    copy_k.wait()
    with jax.named_scope("routing"):
        named = jnp.zeros((ne, tok), F32)
        gate = jnp.zeros((ne, tok), F32)
        for k in range(top):
            hit = routes_ref[k : k + 1, :] == iota((ne, tok), 0)
            named = named + jnp.where(hit, 1.0, 0.0)
            gate = gate + jnp.where(hit, gates_ref[k : k + 1, :], 0.0)
        earlier = jnp.where(iota((tok, tok), 0) < iota((tok, tok), 1), 1.0, 0.0).astype(BF)
        slot = jnp.where(named > 0.5, dot(named.astype(BF), earlier), 100.0)
        token, lane = iota((tok, tiles * tok), 0), iota((tok, tiles * tok), 1)
        repeat = jnp.zeros((tok, tiles * tok), F32)
        offset = jnp.zeros((1, tiles * tok), F32)
        for j in range(tiles):
            repeat = repeat + jnp.where(lane == token + j * tok, 1.0, 0.0)
            offset = offset + jnp.where(lane[0:1, :] >= (j + 1) * tok, float(cap), 0.0)
        repeat = repeat.astype(BF)

        def thirds(x):
            first = x.astype(BF)
            second = (x - first.astype(F32)).astype(BF)
            return first, second, (x - first.astype(F32) - second.astype(F32)).astype(BF)

        slot_4 = dot(slot.astype(BF), repeat) + offset
        gate_4 = sum(dot(g, repeat) for g in thirds(gate))
        spread = iota((peers, GROUP, ne), 2) == iota((peers, GROUP, ne), 0) + reach * peers
        spread = jnp.where(spread, 1.0, 0.0).reshape(span, ne).astype(BF)
        place = iota((peers, GROUP, tiles * tok), 1).reshape(span, tiles * tok).astype(F32)
        takes = dot(spread, slot_4.astype(BF)) == place
        gate_rows = sum(dot(spread, g) for g in thirds(gate_4))
        gate_rows = jnp.sum(jnp.where(takes, gate_rows, 0.0), axis=1, keepdims=True)
        takes = jnp.where(takes, 1.0, 0.0).astype(BF)
        for copy in copy_o:
            copy.wait()
        for copy in copy_os:
            copy.wait_recv()
        send_g[...] = (dot(takes, grads[...]) * gate_rows).astype(BF)

    def group(u):
        return pl.ds(pl.multiple_of(u * GROUP, 16), GROUP)

    own_group = group(me % peers)

    def exchange(src, dst, n):
        def one(i, carry):
            u = (me + i * STRIDE) % peers
            peer = reach * peers + u

            @pl.when(peer != me)
            def _():
                pltpu.make_async_remote_copy(
                    src_ref=src.at[group(u)],
                    dst_ref=dst.at[own_group],
                    send_sem=a2a_send.at[n],
                    recv_sem=a2a_recv.at[n],
                    device_id=(peer, tt),
                    device_id_type=MESH,
                ).start()

            return carry

        lax.fori_loop(0, peers, one, 0)

        @pl.when(core == 0)
        def _():
            dst[own_group, :] = src[own_group, :]

    def exchanged(src, dst, n, wait):
        for c in range(2):

            @pl.when(core == c)
            def _(c=c):
                every = pl.ds(0, span - (1 - c) * GROUP)
                getattr(remote(src.at[every], dst.at[every], a2a_send.at[n], a2a_recv.at[n], other), wait)()

    early = me < peers

    def exchange_far():
        pl.semaphore_wait(barrier, peers)
        exchange(send_g, recv_g, 0)

    @pl.when(core == 0)
    def _():
        exchange(send_g, recv_g, 0)

    @pl.when((core == 1) & jnp.logical_not(early))
    def _():
        exchange_far()


    packed, padded = 16 * cap, 16 * GROUP
    pair, row = lane_groups(16, GROUP)
    compact, expand = [], []
    for j in range(tiles):
        at = row - j * cap
        named_row = jnp.where((at >= 0) & (at < cap), pair * cap + at, -1)
        compact.append(jnp.where(iota((packed, padded), 0) == named_row, 1.0, 0.0).astype(BF))
        at = iota((16, GROUP, packed), 1) - j * cap
        hit = (iota((16, GROUP, packed), 2) == iota((16, GROUP, packed), 0) * cap + at) & (at >= 0) & (at < cap)
        expand.append(jnp.where(hit, 1.0, 0.0).reshape(padded, packed).astype(BF))

    copy_w.wait()
    copy_ws.wait_recv()

    def forward(d, g, first):
        weights = wext.at[(y + ny - d) % ny]
        for side, lanes, depth in ((0, slice(0, 256), slice(pad, pad + 256)), (1, slice(wide - 256, wide), slice(0, 256))):
            out = slice((2 * g + side) * quarter, (2 * g + side + 1) * quarter)
            block = ring[d, g * quarter : (g + 1) * quarter, lanes]
            share = dot(block, weights[depth, :])
            acc[out, :] = share if first else acc[out, :] + share

    def ag_hop(i):
        for way in range(2):
            ag[way][i].wait_recv()
            if i + 2 < ny - 1:
                ag[way][i + 2].start()
        for way in range(2):
            _, dst, which = ag_place(way, i)
            forward(dst, which, False)

    copy_e = remote(acc.at[pl.ds(rows_other, half)], sib_in, sib_send.at[2], sib_recv.at[2], other)

    def give_back():
        copy_e.wait_recv()
        for b in range(peers // 16):
            total = (acc[pl.ds(rows_at + b * packed, packed), :] + sib_in[b * packed : (b + 1) * packed, :]).astype(BF)
            out = sum(dot(expand[j], total[:, j * 128 : (j + 1) * 128]) for j in range(tiles))
            send_e[b * padded : (b + 1) * padded, :] = out.astype(BF)
        exchange(send_e, recv_e, 1)

    forward(0, 0, True)
    forward(0, 1, True)
    for i in range(ny - 3):
        ag_hop(i)
        if i == 0:

            @pl.when((core == 1) & early)
            def _():
                exchange_far()

    exchanged(send_g, recv_g, 0, "wait_recv")
    for b in range(peers // 16):
        arrived = recv_g[b * padded : (b + 1) * padded, :]
        for j in range(tiles):
            rg[pl.ds(rows_at + b * packed, packed), j * 128 : (j + 1) * 128] = dot(compact[j], arrived).astype(BF)
    rg_half = rg.at[pl.ds(rows_at, half)]
    copy_rg = remote(rg_half, rg_half, sib_send.at[1], sib_recv.at[1], other)
    copy_rg.start()

    ag_hop(5)
    def backward(d):
        weights = wext.at[(y + d) % ny]
        for g in range(2):
            out = slice(g * quarter, (g + 1) * quarter)
            low = dot_nt(rg[2 * g * quarter : (2 * g + 1) * quarter, :], weights[pad : pad + 256, :])
            high = dot_nt(rg[(2 * g + 1) * quarter : (2 * g + 2) * quarter, :], weights[0:256, :])
            part[d, out, 0:128] = low[:, 0:128]
            part[d, out, 128:256] = low[:, 128:256] + high[:, 0:128]
            part[d, out, 256:384] = high[:, 128:256]

    far = ny // 2
    rs_place, rs = [], []
    for way in range(2):
        places = [(far, 0, way), (far, 1, way)]
        for step in range(1, far + 1):
            d = (far - step if way == 0 else far + step) % ny
            places += [(d, 0, 1 - way), (d, 1, 1 - way), (d, 0, way), (d, 1, way)]
        rs_place.append(places)
        rs.append({})
        for i, (d, g, which) in enumerate(places):
            if d:
                chunk = pl.ds(0, subs[which][1])
                rs[way][d, g, which] = (
                    i,
                    remote(
                        rs_out.at[way, i, chunk], rs_in.at[way, i, chunk],
                        rs_send.at[way, i], rs_recv.at[way, i], (right, left)[way],
                    ),
                )

    def rs_share(d, g, which):
        first, size = subs[which]
        return part[d, g * quarter + first : g * quarter + first + size, :]

    def rs_arrived(way, d, g, which):
        before = ((d + 1) if way == 0 else (d + ny - 1) % ny, g, which)
        if before not in rs[way]:
            return None
        i, copy = rs[way][before]
        copy.wait_recv()
        return rs_in[way, i, 0 : subs[which][1], :].astype(F32)

    def rs_step(way, n):
        d, g, which = rs_place[way][n]
        arrived = rs_arrived(way, d, g, which)
        total = rs_share(d, g, which)
        if arrived is not None:
            total = total + arrived
        i, copy = rs[way][d, g, which]
        rs_out[way, i, 0 : subs[which][1], :] = total.astype(BF)
        copy.start()

    copy_rg.wait_recv()
    backward(far)
    for n in range(2):
        for way in range(2):
            rs_step(way, n)
    backward(far - 1)
    for n in range(2, 4):
        rs_step(0, n)
    backward(far + 1)
    for n in range(2, 4):
        rs_step(1, n)
    ag_hop(6)
    copy_e.start()
    backward(far - 2)
    backward(far + 2)
    give_back()

    done = {far, far - 1, far + 1, far - 2, far + 2}
    def rs_both(n):
        for way in range(2):
            d = rs_place[way][n][0]
            if d not in done:
                backward(d)
                done.add(d)
            rs_step(way, n)

    for n in range(4, 4 * far - 2):
        rs_both(n)
    backward(0)

    with jax.named_scope("combine"):
        pair, row = lane_groups(peers, GROUP)
        spread_t = jnp.where(iota((ne, span), 0) == pair + reach * peers, 1.0, 0.0).astype(BF)
        takes_t = dot(jnp.transpose(slot_4).astype(BF), spread_t) == row.astype(F32)
        mixing = [jnp.where(takes_t, dot(g, spread_t), 0.0).astype(BF) for g in thirds(jnp.transpose(gate_4))]
    exchanged(send_e, recv_e, 1, "wait_recv")
    arrived = recv_e[...]
    mix_part[...] = dot(mixing[0], arrived) + dot(mixing[1], arrived) + dot(mixing[2], arrived)
    mix_rows = tiles // 2 * tok
    copy_m = remote(
        mix_part.at[pl.ds(pl.multiple_of((1 - core) * mix_rows, 16), mix_rows)], mix_in, sib_send.at[5], sib_recv.at[5], other
    )
    copy_m.start()

    last = {}
    for n in range(4 * far - 2, 4 * far + 2):
        for way in range(2):
            _, g, which = rs_place[way][n]
            if (g, which) not in last:
                last[g, which] = rs_share(0, g, which)
            last[g, which] = last[g, which] + rs_arrived(way, 0, g, which)
    for (g, which), total in last.items():
        first, size = subs[which]
        total = total.astype(BF)
        for side in range(2):
            at = (2 * g + side) * quarter + first
            hgrad_ref[at : at + size, :] = total[:, side * cols : (side + 1) * cols]

    copy_m.wait_recv()
    mixed = (mix_part[pl.ds(pl.multiple_of(core * mix_rows, 16), mix_rows), :] + mix_in[...]).astype(BF)
    for i in range(tiles // 2):
        mixed_ref[:, i * 128 : (i + 1) * 128] = mixed[i * tok : (i + 1) * tok, :]

    for way in range(2):
        for copy in ag[way]:
            copy.wait_send()
        for _, copy in rs[way].values():
            copy.wait_send()
    for copy in (copy_ws, copy_rg, copy_e, copy_m, *copy_os):
        copy.wait_send()
    exchanged(send_g, recv_g, 0, "wait_send")
    exchanged(send_e, recv_e, 1, "wait_send")


def body(routes, gates, hidden, down, out_grad):
    ne, nt = lax.axis_size("expert"), lax.axis_size("tensor")
    ny = nt // 2
    tok, top = routes.shape
    rows, cols = hidden.shape[1:]
    feat = out_grad.shape[1]
    cap = rows // ne
    sizes = (ne, ny, cap, tok, top, rows, cols, feat)
    half, wide = rows // 2, 2 * cols
    sub = (rows // 8 + 15) // 16 * 16
    span = ne // 2 * GROUP
    vmem, hbm = pl.BlockSpec(memory_space=pltpu.VMEM), pl.BlockSpec(memory_space=pltpu.HBM)
    dma = pltpu.SemaphoreType.DMA
    mixed, hgrad = pl.pallas_call(
        functools.partial(kernel, sizes),
        out_shape=(
            jax.ShapeDtypeStruct((tok, feat), BF),
            jax.ShapeDtypeStruct((rows, cols), BF),
        ),
        in_specs=[hbm] * 5,
        out_specs=(vmem, vmem),
        scratch_shapes=[
            pltpu.VMEM((top, tok), jnp.int32),
            pltpu.VMEM((top, tok), F32),
            pltpu.VMEM((feat // 64 * tok, 128), BF),
            pltpu.VMEM((cols, rows), BF),
            pltpu.VMEM((ny, 512 - cols, 2 * feat), BF),
            pltpu.VMEM((ny, half, wide), BF),
            pltpu.VMEM((rows, 2 * feat), F32),
            pltpu.VMEM((half, 2 * feat), F32),
            pltpu.VMEM((rows, 2 * feat), BF),
            pltpu.VMEM((ny, half, wide), F32),
            pltpu.VMEM((2, 2 * ny - 2, sub, wide), BF),
            pltpu.VMEM((2, 2 * ny - 2, sub, wide), BF),
            pltpu.VMEM((span, 128), BF),
            pltpu.VMEM((span, 128), BF),
            pltpu.VMEM((span, 128), BF),
            pltpu.VMEM((span, 128), BF),
            pltpu.VMEM((feat // 64 * tok, 128), F32),
            pltpu.VMEM((feat // 128 * tok, 128), F32),
            pltpu.SemaphoreType.REGULAR,
            dma((4 + feat // 128,)),
            dma((2, ny - 1)),
            dma((2, ny - 1)),
            dma((2, 2 * ny - 2)),
            dma((2, 2 * ny - 2)),
            dma((6,)),
            dma((6,)),
            dma((2,)),
            dma((2,)),
        ],
        compiler_params=pltpu.CompilerParams(
            collective_id=0, has_side_effects=True, vmem_limit_bytes=48 * 1024 * 1024
        ),
    )(*[pltpu.with_memory_space_constraint(a, pltpu.HBM) for a in (routes.T, gates.T, out_grad, hidden[0].T, down.reshape(ny, 2, cols, feat))])
    return mixed, hgrad[None]


def solution(mesh):
    return jax.shard_map(
        body,
        mesh=mesh,
        in_specs=(
            P("expert", None),
            P("expert", None),
            P("expert", None, "tensor"),
            P("expert", None, "tensor"),
            P("expert", "tensor"),
        ),
        out_specs=(P("expert", "tensor"), P("expert", None, "tensor")),
        check_vma=False,
    )
```
